32 devices in a mesh: row: 4 (over y, core), feat: 8 (over z, x).
Axes of the slice: x: 2, y: 2, z: 4, core: 2. Of those that a mesh axis runs over, the one named last changes fastest.
Arguments:
- table_entries: bfloat16 [4096, 128, 128], P('row', 'feat'), may hold values from -6 to 6
- pseudo_points: bfloat16 [2, 128, 128], replicated, may hold values from -6 to 6
- projection_tensors: bfloat16 [2, 2, 4, 128, 128], replicated, may hold values from -0.5 to 0.5
- expanding_linear: bfloat16 [2, 2, 128, 256], replicated, may hold values from -0.5 to 0.5
- contracting_linear: bfloat16 [2, 2, 256, 128], replicated, may hold values from -0.375 to 0.375
- normalizer_multipliers: float32 [2, 4, 128], replicated, may hold values from 0.1 to 1.9
- sharpness_coefficients: float32 [2, 2, 4], replicated, may hold values from 2 to 12
Outputs:
- embedded: bfloat16 [4096, 128, 128], P(('row', 'feat'))
The draws below stay inside these ranges and needn't reach their ends.
All inputs are finite; a program needn't handle non-finite values.
Results may differ from the reference program's by a relative error of at most 0.02.
Values may be sent and summed in bfloat16 or wider, within the bound.
A program may use at most 64 MiB of HBM per device.

```python
import math
import jax
import jax.numpy as jnp
from jax import lax

E = 128
M = 128
FOCUS_CHANNELS = 4
FF = 256
INDUCER_STACKS = 2
COLS = 128
ROWS = 4096


def shard_levels(rng, extent, cuts, low, largest):
    level = 1.0
    for axis_at, shards_of in cuts:
        steps = jax.random.uniform(jax.random.fold_in(jax.random.fold_in(rng, 6), axis_at), (shards_of,), jnp.float32, low / len(cuts), largest / len(cuts))
        level = level * jnp.repeat(jnp.exp(steps), extent[axis_at] // shards_of).reshape((-1,) + (1,) * (len(extent) - 1 - axis_at))
    return level


def noise(key, dims, scale, limit, cuts=(), held_as=jnp.bfloat16):
    gain = shard_levels(key, dims, cuts, -0.22, 0.18) if cuts else 1.0
    entries = jax.random.normal(key, dims, jnp.float32) * scale * gain
    return jnp.minimum(jnp.maximum(entries, -limit), limit).astype(held_as)


def setup_inputs(seed: int = 0) -> dict:
    seeds = jax.random.split(jax.random.key(seed), 8)
    return {
        "table_entries": noise(seeds[0], (ROWS, COLS, E), 1.0, 6.0, ((0, 4), (1, 8))),
        "pseudo_points": noise(seeds[1], (INDUCER_STACKS, M, E), 1.0, 6.0),
        "projection_tensors": noise(seeds[2], (INDUCER_STACKS, 2, 4, E, E), E ** -0.5, 0.5),
        "expanding_linear": noise(seeds[3], (INDUCER_STACKS, 2, E, FF), E ** -0.5, 0.5),
        "contracting_linear": noise(seeds[4], (INDUCER_STACKS, 2, FF, E), FF ** -0.5, 0.375),
        "normalizer_multipliers": jnp.clip(1.0 + 0.18 * jax.random.normal(seeds[5], (INDUCER_STACKS, 4, E), jnp.float32), 0.1, 1.9),
        "sharpness_coefficients": jnp.clip(jnp.exp(jax.random.uniform(seeds[6], (INDUCER_STACKS, 2, FOCUS_CHANNELS), jnp.float32, math.log(2.0), math.log(12.0))), 2.0, 12.0),
    }


def cast_to_half(values):
    return lax.optimization_barrier(values.astype(jnp.bfloat16))

def layer_norm(values, gain_row):
    values = values.astype(jnp.float32)
    center = values - lax.optimization_barrier(jnp.mean(values, axis=-1, keepdims=True))
    spread = lax.optimization_barrier(jnp.mean(center * center, axis=-1, keepdims=True))
    return center * lax.rsqrt(spread + 1e-05) * gain_row

def unit_rms(values):
    return values * lax.rsqrt(lax.optimization_barrier(jnp.mean(values * values, axis=-1, keepdims=True)) + 1e-06)

def partition_channels(values, channel_total):
    return values.reshape(values.shape[0], channel_total, values.shape[1] // channel_total)

def inducing_partials(normed, probe_vectors, key_weight, value_weight, multiplier_list):
    channel_total = multiplier_list.shape[0]
    head_width = probe_vectors.shape[1] // channel_total
    lookup_vectors = cast_to_half(unit_rms(jnp.dot(normed, key_weight, preferred_element_type=jnp.float32)))
    value_matrix_rows = cast_to_half(jnp.dot(normed, value_weight, preferred_element_type=jnp.float32))
    affinity_logits = jnp.einsum('ljc,ejc->jle', partition_channels(probe_vectors, channel_total).astype(jnp.float32), partition_channels(lookup_vectors, channel_total).astype(jnp.float32))
    softmax_weights = jnp.exp(affinity_logits * (multiplier_list / head_width)[:, None, None])
    totals = lax.optimization_barrier(jnp.sum(softmax_weights, axis=2))
    weighted_values = jnp.einsum('qab,bqg->aqg', cast_to_half(softmax_weights).astype(jnp.float32), partition_channels(value_matrix_rows, channel_total).astype(jnp.float32))
    return (totals, weighted_values.reshape(probe_vectors.shape[0], probe_vectors.shape[1]))

def inducing_finish(totals, weighted_values, anchor, out_weight, up_weight, down_weight, gain_mlp, gain_keys, key_weight, value_weight):
    channel_total = totals.shape[0]
    query_count = weighted_values.shape[0]
    blended = weighted_values.reshape(query_count, channel_total, -1) / jnp.transpose(totals)[:, :, None]
    blended = cast_to_half(blended.reshape(query_count, -1))
    summary = anchor.astype(jnp.float32) + jnp.dot(blended, out_weight, preferred_element_type=jnp.float32)
    hidden = cast_to_half(jax.nn.gelu(jnp.dot(cast_to_half(layer_norm(summary, gain_mlp)), up_weight, preferred_element_type=jnp.float32), approximate=True))
    refined = summary + jnp.dot(hidden, down_weight, preferred_element_type=jnp.float32)
    normed = cast_to_half(layer_norm(refined, gain_keys))
    lookup_vectors = cast_to_half(unit_rms(jnp.dot(normed, key_weight, preferred_element_type=jnp.float32)))
    value_matrix_rows = cast_to_half(jnp.dot(normed, value_weight, preferred_element_type=jnp.float32))
    return (lookup_vectors, value_matrix_rows)

def row_side(current, normed, lookup_vectors, value_matrix_rows, query_weight, out_weight, up_weight, down_weight, gain_mlp, multiplier_list):
    channel_total = multiplier_list.shape[0]
    head_width = lookup_vectors.shape[1] // channel_total
    probe_vectors = cast_to_half(unit_rms(jnp.dot(normed, query_weight, preferred_element_type=jnp.float32)))
    affinity_logits = jnp.einsum('lgu,bgu->lgb', partition_channels(probe_vectors, channel_total).astype(jnp.float32), partition_channels(lookup_vectors, channel_total).astype(jnp.float32))
    softmax_weights = jnp.exp(affinity_logits * (multiplier_list / head_width)[None, :, None])
    softmax_weights = cast_to_half(softmax_weights / lax.optimization_barrier(jnp.sum(softmax_weights, axis=2, keepdims=True)))
    attended_rows = jnp.einsum('gql,lqv->gqv', softmax_weights.astype(jnp.float32), partition_channels(value_matrix_rows, channel_total).astype(jnp.float32))
    attended_rows = cast_to_half(attended_rows.reshape(current.shape[0], -1))
    updated = current.astype(jnp.float32) + jnp.dot(attended_rows, out_weight, preferred_element_type=jnp.float32)
    hidden = cast_to_half(jax.nn.gelu(jnp.dot(cast_to_half(layer_norm(updated, gain_mlp)), up_weight, preferred_element_type=jnp.float32), approximate=True))
    updated = updated + jnp.dot(hidden, down_weight, preferred_element_type=jnp.float32)
    return updated.astype(jnp.bfloat16)

def reference(table_entries, pseudo_points, projection_tensors, expanding_linear, contracting_linear, normalizer_multipliers, sharpness_coefficients):

    def one_column(column):
        current = column
        for stack_position in range(INDUCER_STACKS):
            gain_rows = normalizer_multipliers[stack_position]
            multiplier_list = sharpness_coefficients[stack_position]
            weights_ind = projection_tensors[stack_position, 0]
            weights_row = projection_tensors[stack_position, 1]
            normed = cast_to_half(layer_norm(current, gain_rows[0]))
            probe_vectors = cast_to_half(unit_rms(jnp.dot(pseudo_points[stack_position], weights_ind[0], preferred_element_type=jnp.float32)))
            totals, weighted_values = inducing_partials(normed, probe_vectors, weights_ind[1], weights_ind[2], multiplier_list[0])
            lookup_vectors, value_matrix_rows = inducing_finish(totals, weighted_values, pseudo_points[stack_position], weights_ind[3], expanding_linear[stack_position, 0], contracting_linear[stack_position, 0], gain_rows[2], gain_rows[1], weights_row[1], weights_row[2])
            current = row_side(current, normed, lookup_vectors, value_matrix_rows, weights_row[0], weights_row[3], expanding_linear[stack_position, 1], contracting_linear[stack_position, 1], gain_rows[3], multiplier_list[1])
        return current
    columns = lax.map(one_column, jnp.swapaxes(table_entries, 0, 1))
    return jnp.swapaxes(columns, 0, 1)
```

```python
import functools
import math

import jax
import jax.numpy as jnp
from jax import lax
from jax.experimental import pallas as pl
from jax.experimental.pallas import tpu as pltpu
from jax.sharding import PartitionSpec as P

GROUP = 2
CHUNK = 512
MESH = pl.DeviceIdType.MESH
F32, BF16 = jnp.float32, jnp.bfloat16


def dot(a, b):
    return jnp.dot(a, b, preferred_element_type=F32)


def dot_nt(a, b):
    return lax.dot_general(a, b, (((1,), (1,)), ((), ())), preferred_element_type=F32)


def dot_tn(a, b):
    return lax.dot_general(a, b, (((0,), (0,)), ((), ())), preferred_element_type=F32)


def layer_norm(values, gain_row):
    center = values - jnp.mean(values, axis=-1, keepdims=True)
    spread = jnp.mean(center * center, axis=-1, keepdims=True)
    return (center * lax.rsqrt(spread + 1e-05) * gain_row).astype(BF16)


def unit_rms(values):
    return values * lax.rsqrt(jnp.mean(values * values, axis=-1, keepdims=True) + 1e-06)


def gelu(x):
    c = math.sqrt(2.0 / math.pi)
    return (0.5 * x) * (1.0 + jnp.tanh(x * (c + (c * 0.044715) * (x * x))))


def kernel(
    heads,
    x_ref,
    points_ref,
    proj_ref,
    up_ref,
    down_ref,
    gain_ref,
    sharp_ref,
    out_ref,
    state,
    final,
    queries,
    probes,
    wkvq,
    wkv2,
    weights_t,
    values_aug,
    keys_bd,
    values_bd,
    part,
    row_send,
    row_recv,
    out_send,
    out_recv,
    own_sem,
):
    layers = points_ref.shape[0]
    m, e = points_ref.shape[1], points_ref.shape[2]
    cols, rows = x_ref.shape[0], x_ref.shape[1]
    nrow, nfeat = part.shape[2], out_recv.shape[1]
    groups = cols // GROUP
    block = rows // nfeat
    width = e // heads
    me_r, me_f = lax.axis_index("row"), lax.axis_index("feat")

    def row_peer(d):
        return (lax.rem(me_r + d, nrow), me_f)

    def feat_peer(d):
        return (me_r, lax.rem(me_f + d, nfeat))

    barrier = pltpu.get_barrier_semaphore()
    for d in range(1, nrow):
        pl.semaphore_signal(barrier, inc=1, device_id=row_peer(d), device_id_type=MESH)
    for d in range(1, nfeat):
        pl.semaphore_signal(barrier, inc=1, device_id=feat_peer(d), device_id_type=MESH)

    def lane_head(shape):
        return lax.broadcasted_iota(jnp.int32, shape, 1) // width

    def head_mask(h, shape):
        return lane_head(shape) == h

    def lane_scale(b, side):
        lanes = lane_head((1, e))
        scale = jnp.zeros((1, e), F32)
        for h in range(heads):
            scale = jnp.where(lanes == h, sharp_ref[b, side, h], scale)
        return scale * (math.log2(math.e) / width)

    for b in range(layers):
        for at, (side, which) in enumerate(((0, 1), (0, 2), (1, 0))):
            wkvq[b, :, at * e : (at + 1) * e] = proj_ref[b, side, which]
        for at, (side, which) in enumerate(((1, 1), (1, 2))):
            wkv2[b, :, at * e : (at + 1) * e] = proj_ref[b, side, which]
        probe = unit_rms(dot(points_ref[b], proj_ref[b, 0, 0])) * lane_scale(b, 0)
        for h in range(heads):
            probes[b, h * m : (h + 1) * m, :] = jnp.where(
                head_mask(h, (m, e)), probe, 0.0
            ).astype(BF16)
    for g in range(GROUP):
        for h in range(heads):
            values_bd[g, h * m : (h + 1) * m, e:] = head_mask(h, (m, e)).astype(F32).astype(BF16)
    values_aug[:, e:] = jnp.ones((values_aug.shape[0], e), BF16)
    select_row = lax.broadcasted_iota(jnp.int32, (16, e), 0)
    select_lane = lax.broadcasted_iota(jnp.int32, (16, e), 1)
    select = (select_lane == select_row * width).astype(F32).astype(BF16)
    spread = (select_lane // width == select_row).astype(F32).astype(BF16)

    pl.semaphore_wait(barrier, nrow - 1 + nfeat - 1)

    def by_head(stacked):
        total = stacked[:m]
        for h in range(1, heads):
            total = jnp.where(head_mask(h, (m, e)), stacked[h * m : (h + 1) * m], total)
        return total

    def partial_chunk(b, c, at, current):
        normed = layer_norm(current, gain_ref[b, 0][None, :])
        mixed = dot(normed, wkvq[b])
        keys = unit_rms(mixed[:, :e]).astype(BF16)
        values_aug[:, :e] = mixed[:, e : 2 * e].astype(BF16)
        queries[c, pl.ds(at, CHUNK), :] = unit_rms(mixed[:, 2 * e :]).astype(BF16)
        weights_t[...] = jnp.exp2(dot_nt(probes[b], keys)).astype(BF16)
        stacked = dot(weights_t[...], values_aug[...])
        return by_head(stacked[:, :e]), by_head(stacked[:, e:])

    def row_copy(b, t, d):
        return pltpu.make_async_remote_copy(
            src_ref=part.at[b, t, 0],
            dst_ref=part.at[b, t, d],
            send_sem=row_send.at[b, t, d],
            recv_sem=row_recv.at[b, t, d],
            device_id=row_peer(d),
            device_id_type=MESH,
        )

    def send_partials(b, t, g, weighted, totals):
        part[b, t, 0, g, :m, :] = weighted.astype(BF16)
        part[b, t, 0, g, m:, :] = dot_nt(select, totals.astype(BF16)).astype(BF16)

    def finish(b, t):
        for d in range(1, nrow):
            copy = row_copy(b, t, d)
            copy.wait_send()
            copy.wait_recv()
        blended = []
        for g in range(GROUP):
            total = part[b, t, 0, g].astype(F32)
            for d in range(1, nrow):
                total = total + part[b, t, d, g].astype(F32)
            inverse = 1.0 / jnp.where(select_row < heads, total[m:], 1.0)
            high = inverse.astype(BF16)
            low = (inverse - high.astype(F32)).astype(BF16)
            scale = dot_tn(high, spread) + dot_tn(low, spread)
            blended.append((total[:m] * scale).astype(BF16))
        blended = jnp.concatenate(blended, axis=0)
        anchor = jnp.concatenate([points_ref[b].astype(F32)] * GROUP, axis=0)
        summary = anchor + dot(blended, proj_ref[b, 0, 3])
        hidden = gelu(dot(layer_norm(summary, gain_ref[b, 2][None, :]), up_ref[b, 0])).astype(BF16)
        refined = summary + dot(hidden, down_ref[b, 0])
        normed = layer_norm(refined, gain_ref[b, 1][None, :])
        mixed = dot(normed, wkv2[b])
        keys = unit_rms(mixed[:, :e]) * lane_scale(b, 1)
        for g in range(GROUP):
            key = keys[g * m : (g + 1) * m]
            value = mixed[g * m : (g + 1) * m, e:]
            for h in range(heads):
                mask = head_mask(h, (m, e))
                keys_bd[g, h * m : (h + 1) * m, :] = jnp.where(mask, key, 0.0).astype(BF16)
                values_bd[g, h * m : (h + 1) * m, :e] = jnp.where(mask, value, 0.0).astype(BF16)

    def row_chunk(b, g, c, at, current):
        weights = jnp.exp2(dot_nt(queries[c, pl.ds(at, CHUNK), :], keys_bd[g])).astype(BF16)
        both = dot(weights, values_bd[g])
        attended = (both[:, :e] / both[:, e:]).astype(BF16)
        updated = current + dot(attended, proj_ref[b, 1, 3])
        hidden = gelu(dot(layer_norm(updated, gain_ref[b, 3][None, :]), up_ref[b, 1])).astype(BF16)
        return (updated + dot(hidden, down_ref[b, 1])).astype(BF16)

    chunks = rows // CHUNK

    def stage(b, t):
        if b > 0:
            finish(b - 1, t)

        def column(g, carry):
            c = t * GROUP + g
            source = x_ref if b <= 1 else state

            def step(i, sums):
                at = pl.multiple_of(i * CHUNK, CHUNK)
                current = source[c, pl.ds(at, CHUNK), :].astype(F32)
                if b > 0:
                    new = row_chunk(b - 1, g, c, at, current)
                    if b == layers:
                        final[c, pl.ds(at, CHUNK), :] = new
                        return sums
                    state[c, pl.ds(at, CHUNK), :] = new
                    current = new.astype(F32)
                weighted, totals = partial_chunk(b, c, at, current)
                return sums[0] + weighted, sums[1] + totals

            if b == layers:
                lax.fori_loop(0, chunks, step, 0)
            else:
                zero = jnp.zeros((m, e), F32)
                weighted, totals = lax.fori_loop(0, chunks, step, (zero, zero))
                send_partials(b, t, g, weighted, totals)
            return carry

        lax.fori_loop(0, GROUP, column, 0)
        if b < layers:
            for d in range(1, nrow):
                row_copy(b, t, d).start()
        else:
            for d in range(1, nfeat):
                out_copy(t, d).start()
            own_copy(t).start()

    def out_copy(t, d):
        k = lax.rem(me_f + d, nfeat)
        return pltpu.make_async_remote_copy(
            src_ref=final.at[pl.ds(t * GROUP, GROUP), pl.ds(k * block, block)],
            dst_ref=out_ref.at[pl.ds(me_f * cols + t * GROUP, GROUP)],
            send_sem=out_send.at[t, d],
            recv_sem=out_recv.at[t, d],
            device_id=feat_peer(d),
            device_id_type=MESH,
        )

    def own_copy(t):
        return pltpu.make_async_copy(
            final.at[pl.ds(t * GROUP, GROUP), pl.ds(me_f * block, block)],
            out_ref.at[pl.ds(me_f * cols + t * GROUP, GROUP)],
            own_sem.at[t],
        )

    def turn(s, carry):
        for b in range(layers + 1):
            t = s - b

            @pl.when(jnp.logical_and(t >= 0, t < groups))
            def _():
                stage(b, t)

        return carry

    lax.fori_loop(0, groups + layers, turn, 0)

    def drain(t, carry):
        for d in range(1, nfeat):
            out_copy(t, d).wait_send()
            source = lax.rem(me_f + nfeat - d, nfeat)
            pltpu.make_async_remote_copy(
                src_ref=final.at[pl.ds(t * GROUP, GROUP), pl.ds(me_f * block, block)],
                dst_ref=out_ref.at[pl.ds(source * cols + t * GROUP, GROUP)],
                send_sem=out_send.at[t, d],
                recv_sem=out_recv.at[t, d],
                device_id=feat_peer(d),
                device_id_type=MESH,
            ).wait_recv()
        own_copy(t).wait()
        return carry

    lax.fori_loop(0, groups, drain, 0)


def body(
    table_entries,
    pseudo_points,
    projection_tensors,
    expanding_linear,
    contracting_linear,
    normalizer_multipliers,
    sharpness_coefficients,
    *,
    nrow,
    nfeat,
):
    rows, cols, e = table_entries.shape
    layers, m = pseudo_points.shape[:2]
    heads = sharpness_coefficients.shape[2]
    groups = cols // GROUP
    vmem = pl.BlockSpec(memory_space=pltpu.VMEM)
    columns = pl.pallas_call(
        functools.partial(kernel, heads),
        out_shape=jax.ShapeDtypeStruct((cols * nfeat, rows // nfeat, e), BF16),
        in_specs=[vmem] * 6 + [pl.BlockSpec(memory_space=pltpu.SMEM)],
        out_specs=pl.BlockSpec(memory_space=pl.ANY),
        scratch_shapes=[
            pltpu.VMEM((cols, rows, e), BF16),
            pltpu.VMEM((cols, rows, e), BF16),
            pltpu.VMEM((cols, rows, e), BF16),
            pltpu.VMEM((layers, heads * m, e), BF16),
            pltpu.VMEM((layers, e, 3 * e), BF16),
            pltpu.VMEM((layers, e, 2 * e), BF16),
            pltpu.VMEM((heads * m, CHUNK), BF16),
            pltpu.VMEM((CHUNK, 2 * e), BF16),
            pltpu.VMEM((GROUP, heads * m, e), BF16),
            pltpu.VMEM((GROUP, heads * m, 2 * e), BF16),
            pltpu.VMEM((layers, groups, nrow, GROUP, m + 16, e), BF16),
            pltpu.SemaphoreType.DMA((layers, groups, nrow)),
            pltpu.SemaphoreType.DMA((layers, groups, nrow)),
            pltpu.SemaphoreType.DMA((groups, nfeat)),
            pltpu.SemaphoreType.DMA((groups, nfeat)),
            pltpu.SemaphoreType.DMA((groups,)),
        ],
        compiler_params=pltpu.CompilerParams(
            collective_id=0, has_side_effects=True, vmem_limit_bytes=56 * 2**20
        ),
    )(
        jnp.swapaxes(table_entries, 0, 1),
        pseudo_points,
        projection_tensors,
        expanding_linear,
        contracting_linear,
        normalizer_multipliers,
        sharpness_coefficients,
    )
    return jnp.swapaxes(columns, 0, 1)


def solution(mesh):
    return jax.shard_map(
        functools.partial(body, nrow=mesh.shape["row"], nfeat=mesh.shape["feat"]),
        mesh=mesh,
        in_specs=(P("row", "feat", None), P(), P(), P(), P(), P(), P()),
        out_specs=P(("row", "feat"), None, None),
        check_vma=False,
    )
```

```python
import functools
import math

import jax
import jax.numpy as jnp
from jax import lax
from jax.experimental import pallas as pl
from jax.experimental.pallas import tpu as pltpu
from jax.sharding import PartitionSpec as P

CHUNK = 256
MESH = pl.DeviceIdType.MESH
F32, BF16 = jnp.float32, jnp.bfloat16


def dot(a, b):
    return jnp.dot(a, b, preferred_element_type=F32)


def dot_nt(a, b):
    return lax.dot_general(a, b, (((1,), (1,)), ((), ())), preferred_element_type=F32)


def dot_tn(a, b):
    return lax.dot_general(a, b, (((0,), (0,)), ((), ())), preferred_element_type=F32)


def layer_norm(values, gain_row):
    center = values - jnp.mean(values, axis=-1, keepdims=True)
    spread = jnp.mean(center * center, axis=-1, keepdims=True)
    return (center * lax.rsqrt(spread + 1e-05) * gain_row).astype(BF16)


def unit_rms(values):
    return values * lax.rsqrt(jnp.mean(values * values, axis=-1, keepdims=True) + 1e-06)


def gelu(x):
    c = math.sqrt(2.0 / math.pi)
    return (0.5 * x) * (1.0 + jnp.tanh(x * (c + (c * 0.044715) * (x * x))))


def interleave(chains):
    chains = list(chains)
    while chains:
        for chain in list(chains):
            try:
                next(chain)
            except StopIteration:
                chains.remove(chain)


def kernel(
    heads,
    x_ref,
    points_ref,
    proj_ref,
    up_ref,
    down_ref,
    gain_ref,
    sharp_ref,
    out_ref,
    state,
    final,
    queries,
    probes,
    wkvq,
    wkv2,
    scales,
    sums,
    keys_bd,
    values_bd,
    part,
    row_send,
    row_recv,
    out_send,
    out_recv,
    own_sem,
):
    layers = points_ref.shape[0]
    m, e = points_ref.shape[1], points_ref.shape[2]
    cols, rows = x_ref.shape[0], x_ref.shape[1]
    nrow, nfeat = part.shape[2], out_recv.shape[1]
    block = rows // nfeat
    width = e // heads
    chunks = rows // CHUNK
    slab = m // chunks
    me_r, me_f = lax.axis_index("row"), lax.axis_index("feat")

    def row_peer(d):
        return (lax.rem(me_r + d, nrow), me_f)

    def feat_peer(d):
        return (me_r, lax.rem(me_f + d, nfeat))

    barrier = pltpu.get_barrier_semaphore()
    for d in range(1, nrow):
        pl.semaphore_signal(barrier, inc=1, device_id=row_peer(d), device_id_type=MESH)
    for d in range(1, nfeat):
        pl.semaphore_signal(barrier, inc=1, device_id=feat_peer(d), device_id_type=MESH)

    def head_mask(h, shape):
        return lax.broadcasted_iota(jnp.int32, shape, 1) // width == h

    def lane_scale(b, side):
        scale = jnp.zeros((1, e), F32)
        for h in range(heads):
            scale = jnp.where(head_mask(h, (1, e)), sharp_ref[b, side, h], scale)
        return scale * (math.log2(math.e) / width)

    for b in range(layers):
        for at, (side, which) in enumerate(((0, 1), (0, 2), (1, 0))):
            wkvq[b, :, at * e : (at + 1) * e] = proj_ref[b, side, which]
        for at, (side, which) in enumerate(((1, 1), (1, 2))):
            wkv2[b, :, at * e : (at + 1) * e] = proj_ref[b, side, which]
        probe = unit_rms(dot(points_ref[b], proj_ref[b, 0, 0])) * lane_scale(b, 0)
        for h in range(heads):
            mask = head_mask(h, (m, e))
            probes[b, h * m : (h + 1) * m, :] = jnp.where(mask, probe, 0.0).astype(BF16)
            for slot in range(2):
                values_bd[b, slot, h * m : (h + 1) * m, e:] = mask.astype(F32).astype(BF16)

    pl.semaphore_wait(barrier, nrow - 1 + nfeat - 1)

    def select_spread():
        row = lax.broadcasted_iota(jnp.int32, (16, e), 0)
        lane = lax.broadcasted_iota(jnp.int32, (16, e), 1)
        select = (lane == row * width).astype(F32).astype(BF16)
        spread = (lane // width == row).astype(F32).astype(BF16)
        return row, select, spread

    def by_head(stacked):
        total = stacked[:m]
        for h in range(1, heads):
            total = jnp.where(head_mask(h, (m, e)), stacked[h * m : (h + 1) * m], total)
        return total

    def partial_steps(b, c, at, current):
        normed = layer_norm(current, gain_ref[b, 0][None, :])
        yield
        mixed = dot(normed, wkvq[b])
        values = mixed[:, e : 2 * e].astype(BF16)
        values = jnp.concatenate([values, jnp.ones((CHUNK, e), BF16)], axis=1)
        yield
        keys = unit_rms(mixed[:, :e]).astype(BF16)
        yield
        queries[c, pl.ds(at, CHUNK), :] = unit_rms(mixed[:, 2 * e :]).astype(BF16)
        yield
        weights = jnp.exp2(dot_nt(probes[b], keys)).astype(BF16)
        yield
        stacked = dot(weights, values)
        yield
        sums[b, 0] += by_head(stacked[:, :e])
        sums[b, 1] += by_head(stacked[:, e:])

    def row_steps(b, c, at, current, result):
        slot = lax.rem(c, 2)
        query = queries[c, pl.ds(at, CHUNK), :]
        half = heads * m // 2
        weights = []
        for k in range(2):
            logits = dot_nt(query, keys_bd[b, slot, k * half : (k + 1) * half])
            weights.append(jnp.exp2(logits).astype(BF16))
            yield
        both = dot(jnp.concatenate(weights, axis=1), values_bd[b, slot])
        yield
        attended = (both[:, :e] * pl.reciprocal(both[:, e:], approx=True)).astype(BF16)
        yield
        updated = current + dot(attended, proj_ref[b, 1, 3])
        yield
        normed = layer_norm(updated, gain_ref[b, 3][None, :])
        yield
        hidden = gelu(dot(normed, up_ref[b, 1])).astype(BF16)
        yield
        result.append((updated + dot(hidden, down_ref[b, 1])).astype(BF16))

    def chunk_steps(b, c, at):
        source = x_ref if b <= 1 else state
        current = source[c, pl.ds(at, CHUNK), :].astype(F32)
        if b > 0:
            result = []
            yield from row_steps(b - 1, c, at, current, result)
            if b == layers:
                final[c, pl.ds(at, CHUNK), :] = result[0]
                return
            state[c, pl.ds(at, CHUNK), :] = result[0]
            current = result[0].astype(F32)
            yield
        yield from partial_steps(b, c, at, current)

    def row_copy(b, c, d):
        return pltpu.make_async_remote_copy(
            src_ref=part.at[b, c, 0],
            dst_ref=part.at[b, c, d],
            send_sem=row_send.at[b, c, d],
            recv_sem=row_recv.at[b, c, d],
            device_id=row_peer(d),
            device_id_type=MESH,
        )

    def finish_steps(b, c, i):
        slot = lax.rem(c, 2)
        first = pl.multiple_of(i * slab, slab)
        row, _, spread = select_spread()
        total = part[b, c, 0, m:, :].astype(F32)
        for d in range(1, nrow):
            total = total + part[b, c, d, m:, :].astype(F32)
        inverse = 1.0 / jnp.where(row < heads, total, 1.0)
        high = inverse.astype(BF16)
        low = (inverse - high.astype(F32)).astype(BF16)
        yield
        scales[b] = dot_tn(high, spread) + dot_tn(low, spread)
        yield
        total = part[b, c, 0, pl.ds(first, slab), :].astype(F32)
        for d in range(1, nrow):
            total = total + part[b, c, d, pl.ds(first, slab), :].astype(F32)
        blended = (total * scales[b, pl.ds(first, slab), :]).astype(BF16)
        yield
        anchor = points_ref[b, pl.ds(first, slab), :].astype(F32)
        summary = anchor + dot(blended, proj_ref[b, 0, 3])
        yield
        normed = layer_norm(summary, gain_ref[b, 2][None, :])
        yield
        hidden = gelu(dot(normed, up_ref[b, 0])).astype(BF16)
        yield
        refined = summary + dot(hidden, down_ref[b, 0])
        yield
        normed = layer_norm(refined, gain_ref[b, 1][None, :])
        yield
        mixed = dot(normed, wkv2[b])
        yield
        keys = unit_rms(mixed[:, :e]) * lane_scale(b, 1)
        values = mixed[:, e:]
        for h in range(heads):
            mask = head_mask(h, (slab, e))
            at = pl.ds(pl.multiple_of(h * m + i * slab, slab), slab)
            keys_bd[b, slot, at, :] = jnp.where(mask, keys, 0.0).astype(BF16)
            values_bd[b, slot, at, :e] = jnp.where(mask, values, 0.0).astype(BF16)

    def out_copy(c, d):
        k = lax.rem(me_f + d, nfeat)
        return pltpu.make_async_remote_copy(
            src_ref=final.at[c, pl.ds(k * block, block)],
            dst_ref=out_ref.at[me_f * cols + c],
            send_sem=out_send.at[c, d],
            recv_sem=out_recv.at[c, d],
            device_id=feat_peer(d),
            device_id_type=MESH,
        )

    def own_copy(c):
        return pltpu.make_async_copy(
            final.at[c, pl.ds(me_f * block, block)],
            out_ref.at[me_f * cols + c],
            own_sem.at[c],
        )

    jobs = []
    for b in range(layers + 1):
        jobs.append((3 * b, "stage", b))
        if b < layers:
            jobs.append((3 * b + 2, "finish", b))

    def turn(active, s):
        for lag, kind, b in active:
            if kind == "finish":
                for d in range(1, nrow):
                    copy = row_copy(b, s - lag, d)
                    copy.wait_send()
                    copy.wait_recv()
            elif b < layers:
                sums[b] = jnp.zeros((2, m, e), F32)

        def step(i, carry):
            at = pl.multiple_of(i * CHUNK, CHUNK)
            interleave(
                chunk_steps(b, s - lag, at) if kind == "stage" else finish_steps(b, s - lag, i)
                for lag, kind, b in active
            )
            return carry

        lax.fori_loop(0, chunks, step, 0)
        for lag, kind, b in active:
            c = s - lag
            if kind == "finish":
                continue
            if b < layers:
                _, select, _ = select_spread()
                part[b, c, 0, :m, :] = sums[b, 0].astype(BF16)
                part[b, c, 0, m:, :] = dot_nt(select, sums[b, 1].astype(BF16)).astype(BF16)
                for d in range(1, nrow):
                    row_copy(b, c, d).start()
            else:
                for d in range(1, nfeat):
                    out_copy(c, d).start()
                own_copy(c).start()

    turns = [
        tuple(job for job in jobs if 0 <= s - job[0] < cols) for s in range(cols + 3 * layers)
    ]
    s = 0
    while s < len(turns):
        end = s
        while end < len(turns) and turns[end] == turns[s]:
            end += 1
        active = turns[s]

        def run(at, carry, active=active):
            turn(active, at)
            return carry

        lax.fori_loop(s, end, run, 0)
        s = end

    def drain(c, carry):
        for d in range(1, nfeat):
            out_copy(c, d).wait_send()
            source = lax.rem(me_f + nfeat - d, nfeat)
            pltpu.make_async_remote_copy(
                src_ref=final.at[c, pl.ds(me_f * block, block)],
                dst_ref=out_ref.at[source * cols + c],
                send_sem=out_send.at[c, d],
                recv_sem=out_recv.at[c, d],
                device_id=feat_peer(d),
                device_id_type=MESH,
            ).wait_recv()
        own_copy(c).wait()
        return carry

    lax.fori_loop(0, cols, drain, 0)


def body(
    table_entries,
    pseudo_points,
    projection_tensors,
    expanding_linear,
    contracting_linear,
    normalizer_multipliers,
    sharpness_coefficients,
    *,
    nrow,
    nfeat,
):
    rows, cols, e = table_entries.shape
    layers, m = pseudo_points.shape[:2]
    heads = sharpness_coefficients.shape[2]
    vmem = pl.BlockSpec(memory_space=pltpu.VMEM)
    columns = pl.pallas_call(
        functools.partial(kernel, heads),
        out_shape=jax.ShapeDtypeStruct((cols * nfeat, rows // nfeat, e), BF16),
        in_specs=[vmem] * 6 + [pl.BlockSpec(memory_space=pltpu.SMEM)],
        out_specs=pl.BlockSpec(memory_space=pl.ANY),
        scratch_shapes=[
            pltpu.VMEM((cols, rows, e), BF16),
            pltpu.VMEM((cols, rows, e), BF16),
            pltpu.VMEM((cols, rows, e), BF16),
            pltpu.VMEM((layers, heads * m, e), BF16),
            pltpu.VMEM((layers, e, 3 * e), BF16),
            pltpu.VMEM((layers, e, 2 * e), BF16),
            pltpu.VMEM((layers, m, e), F32),
            pltpu.VMEM((layers, 2, m, e), F32),
            pltpu.VMEM((layers, 2, heads * m, e), BF16),
            pltpu.VMEM((layers, 2, heads * m, 2 * e), BF16),
            pltpu.VMEM((layers, cols, nrow, m + 16, e), BF16),
            pltpu.SemaphoreType.DMA((layers, cols, nrow)),
            pltpu.SemaphoreType.DMA((layers, cols, nrow)),
            pltpu.SemaphoreType.DMA((cols, nfeat)),
            pltpu.SemaphoreType.DMA((cols, nfeat)),
            pltpu.SemaphoreType.DMA((cols,)),
        ],
        compiler_params=pltpu.CompilerParams(
            collective_id=0, has_side_effects=True, vmem_limit_bytes=56 * 2**20
        ),
    )(
        jnp.swapaxes(table_entries, 0, 1),
        pseudo_points,
        projection_tensors,
        expanding_linear,
        contracting_linear,
        normalizer_multipliers,
        sharpness_coefficients,
    )
    return jnp.swapaxes(columns, 0, 1)


def solution(mesh):
    return jax.shard_map(
        functools.partial(body, nrow=mesh.shape["row"], nfeat=mesh.shape["feat"]),
        mesh=mesh,
        in_specs=(P("row", "feat", None), P(), P(), P(), P(), P(), P()),
        out_specs=P(("row", "feat"), None, None),
        check_vma=False,
    )
```

```python
import functools
import math

import jax
import jax.numpy as jnp
from jax import lax
from jax.experimental import pallas as pl
from jax.experimental.pallas import tpu as pltpu
from jax.sharding import PartitionSpec as P

CHUNK = 512
MESH = pl.DeviceIdType.MESH
F32, BF16 = jnp.float32, jnp.bfloat16


def dot(a, b):
    return jnp.dot(a, b, preferred_element_type=F32)


def dot_nt(a, b):
    return lax.dot_general(a, b, (((1,), (1,)), ((), ())), preferred_element_type=F32)


def dot_tn(a, b):
    return lax.dot_general(a, b, (((0,), (0,)), ((), ())), preferred_element_type=F32)


def layer_norm(values, gain_row):
    center = values - jnp.mean(values, axis=-1, keepdims=True)
    spread = jnp.mean(center * center, axis=-1, keepdims=True)
    return (center * lax.rsqrt(spread + 1e-05) * gain_row).astype(BF16)


def unit_rms(values):
    return values * lax.rsqrt(jnp.mean(values * values, axis=-1, keepdims=True) + 1e-06)


def gelu(x):
    c = math.sqrt(2.0 / math.pi)
    x = x.astype(BF16)
    half = BF16(0.5) * x
    return half + half * jnp.tanh(x * (BF16(c) + BF16(c * 0.044715) * (x * x)))


def interleave(chains):
    chains = list(chains)
    while chains:
        for chain in list(chains):
            try:
                next(chain)
            except StopIteration:
                chains.remove(chain)


def kernel(
    heads,
    x_ref,
    points_ref,
    proj_ref,
    up_ref,
    down_ref,
    gain_ref,
    sharp_ref,
    out_ref,
    state,
    final,
    queries,
    probes,
    wkvq,
    wkv2,
    scales,
    sums,
    keys_bd,
    values_bd,
    part,
    row_send,
    row_recv,
    out_send,
    out_recv,
    own_sem,
):
    layers = points_ref.shape[0]
    m, e = points_ref.shape[1], points_ref.shape[2]
    cols, rows = x_ref.shape[0], x_ref.shape[1]
    nrow, nfeat = part.shape[2], out_recv.shape[1]
    block = rows // nfeat
    width = e // heads
    chunks = rows // CHUNK
    slab = m // chunks
    me_r, me_f = lax.axis_index("row"), lax.axis_index("feat")

    def row_peer(d):
        return (lax.rem(me_r + d, nrow), me_f)

    def feat_peer(d):
        return (me_r, lax.rem(me_f + d, nfeat))

    barrier = pltpu.get_barrier_semaphore()
    for d in range(1, nrow):
        pl.semaphore_signal(barrier, inc=1, device_id=row_peer(d), device_id_type=MESH)
    for d in range(1, nfeat):
        pl.semaphore_signal(barrier, inc=1, device_id=feat_peer(d), device_id_type=MESH)

    def head_mask(h, shape):
        return lax.broadcasted_iota(jnp.int32, shape, 1) // width == h

    def lane_scale(b, side):
        scale = jnp.zeros((1, e), F32)
        for h in range(heads):
            scale = jnp.where(head_mask(h, (1, e)), sharp_ref[b, side, h], scale)
        return scale * (math.log2(math.e) / width)

    for b in range(layers):
        for at, (side, which) in enumerate(((0, 1), (0, 2), (1, 0))):
            wkvq[b, :, at * e : (at + 1) * e] = proj_ref[b, side, which]
        for at, (side, which) in enumerate(((1, 1), (1, 2))):
            wkv2[b, :, at * e : (at + 1) * e] = proj_ref[b, side, which]
        probe = unit_rms(dot(points_ref[b], proj_ref[b, 0, 0])) * lane_scale(b, 0)
        for h in range(heads):
            mask = head_mask(h, (m, e))
            probes[b, h * m : (h + 1) * m, :] = jnp.where(mask, probe, 0.0).astype(BF16)
            for slot in range(2):
                values_bd[b, slot, h * m : (h + 1) * m, e:] = mask.astype(F32).astype(BF16)

    pl.semaphore_wait(barrier, nrow - 1 + nfeat - 1)

    def select_spread():
        row = lax.broadcasted_iota(jnp.int32, (16, e), 0)
        lane = lax.broadcasted_iota(jnp.int32, (16, e), 1)
        select = (lane == row * width).astype(F32).astype(BF16)
        spread = (lane // width == row).astype(F32).astype(BF16)
        return row, select, spread

    def by_head(stacked):
        total = stacked[:m]
        for h in range(1, heads):
            total = jnp.where(head_mask(h, (m, e)), stacked[h * m : (h + 1) * m], total)
        return total

    def partial_steps(b, c, at, current):
        normed = layer_norm(current, gain_ref[b, 0][None, :])
        yield
        mixed = dot(normed, wkvq[b])
        values = mixed[:, e : 2 * e].astype(BF16)
        values = jnp.concatenate([values, jnp.ones((CHUNK, e), BF16)], axis=1)
        yield
        keys = unit_rms(mixed[:, :e]).astype(BF16)
        yield
        queries[c, pl.ds(at, CHUNK), :] = unit_rms(mixed[:, 2 * e :]).astype(BF16)
        yield
        weights = jnp.exp2(dot_nt(probes[b], keys).astype(BF16))
        yield
        stacked = dot(weights, values)
        yield
        sums[b, 0] += by_head(stacked[:, :e])
        sums[b, 1] += by_head(stacked[:, e:])

    def row_steps(b, c, at, current, result):
        slot = lax.rem(c, 2)
        query = queries[c, pl.ds(at, CHUNK), :]
        half = heads * m // 2
        weights = []
        for k in range(2):
            logits = dot_nt(query, keys_bd[b, slot, k * half : (k + 1) * half])
            weights.append(jnp.exp2(logits.astype(BF16)))
            yield
        both = dot(jnp.concatenate(weights, axis=1), values_bd[b, slot])
        yield
        attended = (both[:, :e] * pl.reciprocal(both[:, e:], approx=True)).astype(BF16)
        yield
        updated = current + dot(attended, proj_ref[b, 1, 3])
        yield
        normed = layer_norm(updated, gain_ref[b, 3][None, :])
        yield
        hidden = gelu(dot(normed, up_ref[b, 1]))
        yield
        result.append((updated + dot(hidden, down_ref[b, 1])).astype(BF16))

    def chunk_steps(b, c, at):
        source = x_ref if b <= 1 else state
        current = source[c, pl.ds(at, CHUNK), :].astype(F32)
        if b > 0:
            result = []
            yield from row_steps(b - 1, c, at, current, result)
            if b == layers:
                final[c, pl.ds(at, CHUNK), :] = result[0]
                return
            state[c, pl.ds(at, CHUNK), :] = result[0]
            current = result[0].astype(F32)
            yield
        yield from partial_steps(b, c, at, current)

    def row_copy(b, c, d):
        return pltpu.make_async_remote_copy(
            src_ref=part.at[b, c, 0],
            dst_ref=part.at[b, c, d],
            send_sem=row_send.at[b, c, d],
            recv_sem=row_recv.at[b, c, d],
            device_id=row_peer(d),
            device_id_type=MESH,
        )

    def finish_steps(b, c, i):
        slot = lax.rem(c, 2)
        first = pl.multiple_of(i * slab, slab)
        row, _, spread = select_spread()
        total = part[b, c, 0, m:, :].astype(F32)
        for d in range(1, nrow):
            total = total + part[b, c, d, m:, :].astype(F32)
        inverse = 1.0 / jnp.where(row < heads, total, 1.0)
        high = inverse.astype(BF16)
        low = (inverse - high.astype(F32)).astype(BF16)
        yield
        scales[b] = dot_tn(high, spread) + dot_tn(low, spread)
        yield
        total = part[b, c, 0, pl.ds(first, slab), :].astype(F32)
        for d in range(1, nrow):
            total = total + part[b, c, d, pl.ds(first, slab), :].astype(F32)
        blended = (total * scales[b, pl.ds(first, slab), :]).astype(BF16)
        yield
        anchor = points_ref[b, pl.ds(first, slab), :].astype(F32)
        summary = anchor + dot(blended, proj_ref[b, 0, 3])
        yield
        normed = layer_norm(summary, gain_ref[b, 2][None, :])
        yield
        hidden = gelu(dot(normed, up_ref[b, 0]))
        yield
        refined = summary + dot(hidden, down_ref[b, 0])
        yield
        normed = layer_norm(refined, gain_ref[b, 1][None, :])
        yield
        mixed = dot(normed, wkv2[b])
        yield
        keys = unit_rms(mixed[:, :e]) * lane_scale(b, 1)
        values = mixed[:, e:]
        for h in range(heads):
            mask = head_mask(h, (slab, e))
            at = pl.ds(pl.multiple_of(h * m + i * slab, slab), slab)
            keys_bd[b, slot, at, :] = jnp.where(mask, keys, 0.0).astype(BF16)
            values_bd[b, slot, at, :e] = jnp.where(mask, values, 0.0).astype(BF16)

    def out_copy(c, d):
        k = lax.rem(me_f + d, nfeat)
        return pltpu.make_async_remote_copy(
            src_ref=final.at[c, pl.ds(k * block, block)],
            dst_ref=out_ref.at[me_f * cols + c],
            send_sem=out_send.at[c, d],
            recv_sem=out_recv.at[c, d],
            device_id=feat_peer(d),
            device_id_type=MESH,
        )

    def own_copy(c):
        return pltpu.make_async_copy(
            final.at[c, pl.ds(me_f * block, block)],
            out_ref.at[me_f * cols + c],
            own_sem.at[c],
        )

    jobs = []
    for b in range(layers + 1):
        jobs.append((3 * b, "stage", b))
        if b < layers:
            jobs.append((3 * b + 2, "finish", b))

    def turn(active, s):
        for lag, kind, b in active:
            if kind == "finish":
                for d in range(1, nrow):
                    copy = row_copy(b, s - lag, d)
                    copy.wait_send()
                    copy.wait_recv()
            elif b < layers:
                sums[b] = jnp.zeros((2, m, e), F32)

        def step(i, carry):
            at = pl.multiple_of(i * CHUNK, CHUNK)
            interleave(
                chunk_steps(b, s - lag, at) if kind == "stage" else finish_steps(b, s - lag, i)
                for lag, kind, b in active
            )
            return carry

        lax.fori_loop(0, chunks, step, 0)
        for lag, kind, b in active:
            c = s - lag
            if kind == "finish":
                continue
            if b < layers:
                _, select, _ = select_spread()
                part[b, c, 0, :m, :] = sums[b, 0].astype(BF16)
                part[b, c, 0, m:, :] = dot_nt(select, sums[b, 1].astype(BF16)).astype(BF16)
                for d in range(1, nrow):
                    row_copy(b, c, d).start()
            else:
                for d in range(1, nfeat):
                    out_copy(c, d).start()
                own_copy(c).start()

    turns = [
        tuple(job for job in jobs if 0 <= s - job[0] < cols) for s in range(cols + 3 * layers)
    ]
    s = 0
    while s < len(turns):
        end = s
        while end < len(turns) and turns[end] == turns[s]:
            end += 1
        active = turns[s]

        def run(at, carry, active=active):
            turn(active, at)
            return carry

        lax.fori_loop(s, end, run, 0)
        s = end

    def drain(c, carry):
        for d in range(1, nfeat):
            out_copy(c, d).wait_send()
            source = lax.rem(me_f + nfeat - d, nfeat)
            pltpu.make_async_remote_copy(
                src_ref=final.at[c, pl.ds(me_f * block, block)],
                dst_ref=out_ref.at[source * cols + c],
                send_sem=out_send.at[c, d],
                recv_sem=out_recv.at[c, d],
                device_id=feat_peer(d),
                device_id_type=MESH,
            ).wait_recv()
        own_copy(c).wait()
        return carry

    lax.fori_loop(0, cols, drain, 0)


def body(
    table_entries,
    pseudo_points,
    projection_tensors,
    expanding_linear,
    contracting_linear,
    normalizer_multipliers,
    sharpness_coefficients,
    *,
    nrow,
    nfeat,
):
    rows, cols, e = table_entries.shape
    layers, m = pseudo_points.shape[:2]
    heads = sharpness_coefficients.shape[2]
    vmem = pl.BlockSpec(memory_space=pltpu.VMEM)
    columns = pl.pallas_call(
        functools.partial(kernel, heads),
        out_shape=jax.ShapeDtypeStruct((cols * nfeat, rows // nfeat, e), BF16),
        in_specs=[vmem] * 6 + [pl.BlockSpec(memory_space=pltpu.SMEM)],
        out_specs=pl.BlockSpec(memory_space=pl.ANY),
        scratch_shapes=[
            pltpu.VMEM((cols, rows, e), BF16),
            pltpu.VMEM((cols, rows, e), BF16),
            pltpu.VMEM((cols, rows, e), BF16),
            pltpu.VMEM((layers, heads * m, e), BF16),
            pltpu.VMEM((layers, e, 3 * e), BF16),
            pltpu.VMEM((layers, e, 2 * e), BF16),
            pltpu.VMEM((layers, m, e), F32),
            pltpu.VMEM((layers, 2, m, e), F32),
            pltpu.VMEM((layers, 2, heads * m, e), BF16),
            pltpu.VMEM((layers, 2, heads * m, 2 * e), BF16),
            pltpu.VMEM((layers, cols, nrow, m + 16, e), BF16),
            pltpu.SemaphoreType.DMA((layers, cols, nrow)),
            pltpu.SemaphoreType.DMA((layers, cols, nrow)),
            pltpu.SemaphoreType.DMA((cols, nfeat)),
            pltpu.SemaphoreType.DMA((cols, nfeat)),
            pltpu.SemaphoreType.DMA((cols,)),
        ],
        compiler_params=pltpu.CompilerParams(
            collective_id=0, has_side_effects=True, vmem_limit_bytes=56 * 2**20
        ),
    )(
        jnp.swapaxes(table_entries, 0, 1),
        pseudo_points,
        projection_tensors,
        expanding_linear,
        contracting_linear,
        normalizer_multipliers,
        sharpness_coefficients,
    )
    return jnp.swapaxes(columns, 0, 1)


def solution(mesh):
    return jax.shard_map(
        functools.partial(body, nrow=mesh.shape["row"], nfeat=mesh.shape["feat"]),
        mesh=mesh,
        in_specs=(P("row", "feat", None), P(), P(), P(), P(), P(), P()),
        out_specs=P(("row", "feat"), None, None),
        check_vma=False,
    )
```

```python
import functools
import math

import jax
import jax.numpy as jnp
from jax import lax
from jax.experimental import pallas as pl
from jax.experimental.pallas import tpu as pltpu
from jax.sharding import PartitionSpec as P

CHUNK = 512
MESH = pl.DeviceIdType.MESH
F32, BF16 = jnp.float32, jnp.bfloat16


def dot(a, b):
    return jnp.dot(a, b, preferred_element_type=F32)


def dot_nt(a, b):
    return lax.dot_general(a, b, (((1,), (1,)), ((), ())), preferred_element_type=F32)


def dot_tn(a, b):
    return lax.dot_general(a, b, (((0,), (0,)), ((), ())), preferred_element_type=F32)


def layer_norm(values, gain_row):
    center = values - jnp.mean(values, axis=-1, keepdims=True)
    spread = jnp.mean(center * center, axis=-1, keepdims=True)
    return (center * lax.rsqrt(spread + 1e-05) * gain_row).astype(BF16)


def unit_rms(values):
    return values * lax.rsqrt(jnp.mean(values * values, axis=-1, keepdims=True) + 1e-06)


def bare_norm(values):
    e = values.shape[-1]
    center = values - jnp.mean(values, axis=-1, keepdims=True)
    total = jnp.sum(center * center, axis=-1, keepdims=True)
    return (center * lax.rsqrt(total + e * 1e-05)).astype(BF16)


def bare_rms(values):
    total = jnp.sum(values * values, axis=-1, keepdims=True)
    return (values * lax.rsqrt(total + values.shape[-1] * 1e-06)).astype(BF16)


def gelu2(x):
    c = math.sqrt(2.0 / math.pi)
    x = x.astype(BF16)
    return x + x * jnp.tanh(x * (BF16(c) + BF16(c * 0.044715) * (x * x)))


def interleave(chains):
    chains = list(chains)
    while chains:
        for chain in list(chains):
            try:
                next(chain)
            except StopIteration:
                chains.remove(chain)


def kernel(
    heads,
    x_ref,
    points_ref,
    proj_ref,
    up_ref,
    down_ref,
    gain_ref,
    sharp_ref,
    out_ref,
    state,
    final,
    queries,
    probes,
    wkvq,
    wkv2,
    up_row,
    down_half,
    scales,
    sums,
    keys_bd,
    values_bd,
    part,
    row_send,
    row_recv,
    out_send,
    out_recv,
    own_sem,
):
    layers = points_ref.shape[0]
    m, e = points_ref.shape[1], points_ref.shape[2]
    cols, rows = x_ref.shape[0], x_ref.shape[1]
    nrow, nfeat = part.shape[2], out_recv.shape[1]
    block = rows // nfeat
    width = e // heads
    chunks = rows // CHUNK
    slab = m // chunks
    me_r, me_f = lax.axis_index("row"), lax.axis_index("feat")

    def row_peer(d):
        return (lax.rem(me_r + d, nrow), me_f)

    def feat_peer(d):
        return (me_r, lax.rem(me_f + d, nfeat))

    barrier = pltpu.get_barrier_semaphore()
    for d in range(1, nrow):
        pl.semaphore_signal(barrier, inc=1, device_id=row_peer(d), device_id_type=MESH)
    for d in range(1, nfeat):
        pl.semaphore_signal(barrier, inc=1, device_id=feat_peer(d), device_id_type=MESH)

    def head_mask(h, shape):
        return lax.broadcasted_iota(jnp.int32, shape, 1) // width == h

    def lane_scale(b, side):
        scale = jnp.zeros((1, e), F32)
        for h in range(heads):
            scale = jnp.where(head_mask(h, (1, e)), sharp_ref[b, side, h], scale)
        return scale * (math.sqrt(e) * math.log2(math.e) / width)

    def with_gain(gain, weight):
        eye = lax.broadcasted_iota(jnp.int32, (e, e), 0) == lax.broadcasted_iota(
            jnp.int32, (e, e), 1
        )
        column = jnp.sum(jnp.where(eye, gain[None, :], 0.0), axis=1, keepdims=True)
        return (weight.astype(F32) * (column * math.sqrt(e))).astype(BF16)

    for b in range(layers):
        for at, (side, which) in enumerate(((0, 1), (0, 2), (1, 0))):
            wkvq[b, :, at * e : (at + 1) * e] = with_gain(gain_ref[b, 0], proj_ref[b, side, which])
        up_row[b] = with_gain(gain_ref[b, 3], up_ref[b, 1])
        for side in range(2):
            down_half[b, side] = (down_ref[b, side].astype(F32) * 0.5).astype(BF16)
        for at, (side, which) in enumerate(((1, 1), (1, 2))):
            wkv2[b, :, at * e : (at + 1) * e] = proj_ref[b, side, which]
        probe = unit_rms(dot(points_ref[b], proj_ref[b, 0, 0])) * lane_scale(b, 0)
        for h in range(heads):
            mask = head_mask(h, (m, e))
            probes[b, h * m : (h + 1) * m, :] = jnp.where(mask, probe, 0.0).astype(BF16)
            for slot in range(2):
                values_bd[b, slot, h * m : (h + 1) * m, e:] = mask.astype(F32).astype(BF16)

    pl.semaphore_wait(barrier, nrow - 1 + nfeat - 1)

    def select_spread():
        row = lax.broadcasted_iota(jnp.int32, (16, e), 0)
        lane = lax.broadcasted_iota(jnp.int32, (16, e), 1)
        select = (lane == row * width).astype(F32).astype(BF16)
        spread = (lane // width == row).astype(F32).astype(BF16)
        return row, select, spread

    def by_head(stacked):
        total = stacked[:m]
        for h in range(1, heads):
            total = jnp.where(head_mask(h, (m, e)), stacked[h * m : (h + 1) * m], total)
        return total

    def partial_steps(b, c, at, current):
        normed = bare_norm(current)
        yield
        mixed = dot(normed, wkvq[b])
        values = mixed[:, e : 2 * e].astype(BF16)
        values = jnp.concatenate([values, jnp.ones((CHUNK, e), BF16)], axis=1)
        yield
        keys = bare_rms(mixed[:, :e])
        yield
        queries[c, pl.ds(at, CHUNK), :] = bare_rms(mixed[:, 2 * e :])
        yield
        weights = jnp.exp2(dot_nt(probes[b], keys).astype(BF16))
        yield
        stacked = dot(weights, values)
        yield
        sums[b, 0] += by_head(stacked[:, :e])
        sums[b, 1] += by_head(stacked[:, e:])

    def row_steps(b, c, at, current, result):
        slot = lax.rem(c, 2)
        query = queries[c, pl.ds(at, CHUNK), :]
        half = heads * m // 2
        weights = []
        for k in range(2):
            logits = dot_nt(query, keys_bd[b, slot, k * half : (k + 1) * half])
            weights.append(jnp.exp2(logits.astype(BF16)))
            yield
        both = dot(jnp.concatenate(weights, axis=1), values_bd[b, slot])
        yield
        attended = (both[:, :e] * pl.reciprocal(both[:, e:], approx=True)).astype(BF16)
        yield
        updated = current + dot(attended, proj_ref[b, 1, 3])
        yield
        normed = bare_norm(updated)
        yield
        hidden = gelu2(dot(normed, up_row[b]))
        yield
        result.append((updated + dot(hidden, down_half[b, 1])).astype(BF16))

    def chunk_steps(b, c, at):
        source = x_ref if b <= 1 else state
        current = source[c, pl.ds(at, CHUNK), :].astype(F32)
        if b > 0:
            result = []
            yield from row_steps(b - 1, c, at, current, result)
            if b == layers:
                final[c, pl.ds(at, CHUNK), :] = result[0]
                return
            state[c, pl.ds(at, CHUNK), :] = result[0]
            current = result[0].astype(F32)
            yield
        yield from partial_steps(b, c, at, current)

    def row_copy(b, c, d):
        return pltpu.make_async_remote_copy(
            src_ref=part.at[b, c, 0],
            dst_ref=part.at[b, c, d],
            send_sem=row_send.at[b, c, d],
            recv_sem=row_recv.at[b, c, d],
            device_id=row_peer(d),
            device_id_type=MESH,
        )

    def finish_steps(b, c, i):
        slot = lax.rem(c, 2)
        first = pl.multiple_of(i * slab, slab)
        row, _, spread = select_spread()
        total = part[b, c, 0, m:, :].astype(F32)
        for d in range(1, nrow):
            total = total + part[b, c, d, m:, :].astype(F32)
        inverse = 1.0 / jnp.where(row < heads, total, 1.0)
        high = inverse.astype(BF16)
        low = (inverse - high.astype(F32)).astype(BF16)
        yield
        scales[b] = dot_tn(high, spread) + dot_tn(low, spread)
        yield
        total = part[b, c, 0, pl.ds(first, slab), :].astype(F32)
        for d in range(1, nrow):
            total = total + part[b, c, d, pl.ds(first, slab), :].astype(F32)
        blended = (total * scales[b, pl.ds(first, slab), :]).astype(BF16)
        yield
        anchor = points_ref[b, pl.ds(first, slab), :].astype(F32)
        summary = anchor + dot(blended, proj_ref[b, 0, 3])
        yield
        normed = layer_norm(summary, gain_ref[b, 2][None, :])
        yield
        hidden = gelu2(dot(normed, up_ref[b, 0]))
        yield
        refined = summary + dot(hidden, down_half[b, 0])
        yield
        normed = layer_norm(refined, gain_ref[b, 1][None, :])
        yield
        mixed = dot(normed, wkv2[b])
        yield
        keys = unit_rms(mixed[:, :e]) * lane_scale(b, 1)
        values = mixed[:, e:]
        for h in range(heads):
            mask = head_mask(h, (slab, e))
            at = pl.ds(pl.multiple_of(h * m + i * slab, slab), slab)
            keys_bd[b, slot, at, :] = jnp.where(mask, keys, 0.0).astype(BF16)
            values_bd[b, slot, at, :e] = jnp.where(mask, values, 0.0).astype(BF16)

    def out_copy(c, d):
        k = lax.rem(me_f + d, nfeat)
        return pltpu.make_async_remote_copy(
            src_ref=final.at[c, pl.ds(k * block, block)],
            dst_ref=out_ref.at[me_f * cols + c],
            send_sem=out_send.at[c, d],
            recv_sem=out_recv.at[c, d],
            device_id=feat_peer(d),
            device_id_type=MESH,
        )

    def own_copy(c):
        return pltpu.make_async_copy(
            final.at[c, pl.ds(me_f * block, block)],
            out_ref.at[me_f * cols + c],
            own_sem.at[c],
        )

    jobs = []
    for b in range(layers + 1):
        jobs.append((3 * b, "stage", b))
        if b < layers:
            jobs.append((3 * b + 2, "finish", b))

    def turn(active, s):
        for lag, kind, b in active:
            if kind == "finish":
                for d in range(1, nrow):
                    copy = row_copy(b, s - lag, d)
                    copy.wait_send()
                    copy.wait_recv()
            elif b < layers:
                sums[b] = jnp.zeros((2, m, e), F32)

        def step(i, carry):
            at = pl.multiple_of(i * CHUNK, CHUNK)
            interleave(
                chunk_steps(b, s - lag, at) if kind == "stage" else finish_steps(b, s - lag, i)
                for lag, kind, b in active
            )
            return carry

        lax.fori_loop(0, chunks, step, 0)
        for lag, kind, b in active:
            c = s - lag
            if kind == "finish":
                continue
            if b < layers:
                _, select, _ = select_spread()
                part[b, c, 0, :m, :] = sums[b, 0].astype(BF16)
                part[b, c, 0, m:, :] = dot_nt(select, sums[b, 1].astype(BF16)).astype(BF16)
                for d in range(1, nrow):
                    row_copy(b, c, d).start()
            else:
                for d in range(1, nfeat):
                    out_copy(c, d).start()
                own_copy(c).start()

    turns = [
        tuple(job for job in jobs if 0 <= s - job[0] < cols) for s in range(cols + 3 * layers)
    ]
    s = 0
    while s < len(turns):
        end = s
        while end < len(turns) and turns[end] == turns[s]:
            end += 1
        active = turns[s]

        def run(at, carry, active=active):
            turn(active, at)
            return carry

        lax.fori_loop(s, end, run, 0)
        s = end

    def drain(c, carry):
        for d in range(1, nfeat):
            out_copy(c, d).wait_send()
            source = lax.rem(me_f + nfeat - d, nfeat)
            pltpu.make_async_remote_copy(
                src_ref=final.at[c, pl.ds(me_f * block, block)],
                dst_ref=out_ref.at[source * cols + c],
                send_sem=out_send.at[c, d],
                recv_sem=out_recv.at[c, d],
                device_id=feat_peer(d),
                device_id_type=MESH,
            ).wait_recv()
        own_copy(c).wait()
        return carry

    lax.fori_loop(0, cols, drain, 0)


def body(
    table_entries,
    pseudo_points,
    projection_tensors,
    expanding_linear,
    contracting_linear,
    normalizer_multipliers,
    sharpness_coefficients,
    *,
    nrow,
    nfeat,
):
    rows, cols, e = table_entries.shape
    layers, m = pseudo_points.shape[:2]
    heads = sharpness_coefficients.shape[2]
    vmem = pl.BlockSpec(memory_space=pltpu.VMEM)
    columns = pl.pallas_call(
        functools.partial(kernel, heads),
        out_shape=jax.ShapeDtypeStruct((cols * nfeat, rows // nfeat, e), BF16),
        in_specs=[vmem] * 6 + [pl.BlockSpec(memory_space=pltpu.SMEM)],
        out_specs=pl.BlockSpec(memory_space=pl.ANY),
        scratch_shapes=[
            pltpu.VMEM((cols, rows, e), BF16),
            pltpu.VMEM((cols, rows, e), BF16),
            pltpu.VMEM((cols, rows, e), BF16),
            pltpu.VMEM((layers, heads * m, e), BF16),
            pltpu.VMEM((layers, e, 3 * e), BF16),
            pltpu.VMEM((layers, e, 2 * e), BF16),
            pltpu.VMEM((layers,) + expanding_linear.shape[2:], BF16),
            pltpu.VMEM(contracting_linear.shape, BF16),
            pltpu.VMEM((layers, m, e), F32),
            pltpu.VMEM((layers, 2, m, e), F32),
            pltpu.VMEM((layers, 2, heads * m, e), BF16),
            pltpu.VMEM((layers, 2, heads * m, 2 * e), BF16),
            pltpu.VMEM((layers, cols, nrow, m + 16, e), BF16),
            pltpu.SemaphoreType.DMA((layers, cols, nrow)),
            pltpu.SemaphoreType.DMA((layers, cols, nrow)),
            pltpu.SemaphoreType.DMA((cols, nfeat)),
            pltpu.SemaphoreType.DMA((cols, nfeat)),
            pltpu.SemaphoreType.DMA((cols,)),
        ],
        compiler_params=pltpu.CompilerParams(
            collective_id=0, has_side_effects=True, vmem_limit_bytes=56 * 2**20
        ),
    )(
        jnp.swapaxes(table_entries, 0, 1),
        pseudo_points,
        projection_tensors,
        expanding_linear,
        contracting_linear,
        normalizer_multipliers,
        sharpness_coefficients,
    )
    return jnp.swapaxes(columns, 0, 1)


def solution(mesh):
    return jax.shard_map(
        functools.partial(body, nrow=mesh.shape["row"], nfeat=mesh.shape["feat"]),
        mesh=mesh,
        in_specs=(P("row", "feat", None), P(), P(), P(), P(), P(), P()),
        out_specs=P(("row", "feat"), None, None),
        check_vma=False,
    )
```
